32 devices in a mesh: head: 2 (over y), blk: 16 (over z, x, core).
Axes of the slice: x: 2, y: 2, z: 4, core: 2. Of those that a mesh axis runs over, the one named last changes fastest.
Arguments:
- queries: bfloat16 [4096, 6144], P(('blk', 'head')), may hold values from -4.5 to 4.5
- key_states: bfloat16 [4096, 6144], P(('blk', 'head')), may hold values from -4.5 to 4.5
- value_states: bfloat16 [4096, 6144], P(('blk', 'head')), may hold values from -6 to 6
- block_lists: int32 [32, 8], P('blk'), may hold values from 0 to 31, as said below
- block_counts: int32 [32], P('blk'), may hold values from 1 to 8
- tile_order: int32 [32], replicated, may hold values from 0 to 31, each once
Outputs:
- attended: bfloat16 [4096, 6144], P(('blk', 'head'))
The draws below stay inside these ranges and needn't reach their ends.
Inputs may be any that keep to these rules, and one draw needn't show every extreme that they name: `block_lists`: entry 0 of row t is t itself; the entries of a row are distinct, and each names a tile whose shard of 2 tiles lies at most 3 shards from the shard of t, counted cyclically over the clip.
All inputs are finite; a program needn't handle non-finite values.
Results may differ from the reference program's by a relative error of at most 0.0095.
Values may be sent and summed in bfloat16 or wider, within the bound.
A program may use at most 128 MiB of HBM per device.

```python
import jax
import jax.numpy as jnp
from jax import lax

H = 48
DH = 128
TILE = 128
REACH = 3
SLOTS = 8
TPS = 2
SEQ = 4096
NTILES = 32


def make_states(key, which):
    rows = SEQ
    width = H * DH
    own_key = jax.random.fold_in(key, 11 + which)
    base = jnp.clip(jax.random.normal(own_key, (rows, width), jnp.float32), -4.5, 4.5)
    return base.astype(jnp.bfloat16)


def draw_queries(key, part):
    return make_states(key, 0)


def draw_key_states(key, part):
    return make_states(key, 1)


def draw_block_lists(key, part):
    window_tiles = (2 * REACH + 1) * TPS
    shard_total = NTILES // TPS
    tile_index = jnp.arange(NTILES, dtype=jnp.int32)
    row_keys = jax.random.split(jax.random.fold_in(key, 31), NTILES)
    picks = jax.vmap(lambda row_key: jax.random.permutation(row_key, window_tiles - 1))(row_keys)[:, :SLOTS - 1]
    picks = picks.astype(jnp.int32)
    self_place = REACH * TPS + tile_index % TPS
    window_place = picks + (picks >= self_place[:, None]).astype(jnp.int32)
    offset = window_place // TPS - REACH
    local_tile = window_place % TPS
    shard = ((tile_index // TPS)[:, None] + offset) % shard_total
    listed = shard * TPS + local_tile
    return jnp.concatenate([tile_index[:, None], listed], axis=1).astype(jnp.int32)


def draw_block_counts(key, part):
    counts = jax.random.randint(jax.random.fold_in(key, 53), (NTILES,), 1, SLOTS + 1).astype(jnp.int32)
    counts = counts.at[0].set(SLOTS)
    counts = counts.at[1].set(1)
    return counts


def block_scale(stream_key, dims, cuts, low, high):
    gain, own = 1.0, jax.random.fold_in(stream_key, 6)
    for axis_at, shards_of in cuts:
        heights = jnp.exp(jax.random.uniform(jax.random.fold_in(own, axis_at), (shards_of,), jnp.float32, low / len(cuts), high / len(cuts)))
        gain = gain * jnp.repeat(heights, dims[axis_at] // shards_of).reshape([-1 if axis == axis_at else 1 for axis in range(len(dims))])
    return gain


def centred(stream_key, dims, scale, bound, cuts=(), kind=jnp.bfloat16):
    loudness = block_scale(stream_key, dims, cuts, -0.22, 0.18) if cuts else 1.0
    array = jax.random.normal(stream_key, dims, jnp.float32) * scale * loudness
    return jnp.minimum(jnp.maximum(array, -bound), bound).astype(kind)


def setup_inputs(seed: int = 0) -> dict:
    key_list = jax.random.split(jax.random.key(seed), 7)
    queries = draw_queries(jax.random.fold_in(key_list[6], 71), 0)
    key_states = draw_key_states(jax.random.fold_in(key_list[6], 71), 0)
    value_states = centred(key_list[2], (SEQ, H * DH), 1.0, 6.0, ((0, 32),))
    block_lists = draw_block_lists(jax.random.fold_in(key_list[6], 71), 0)
    block_counts = draw_block_counts(jax.random.fold_in(key_list[6], 71), 0)
    tile_order = jax.random.permutation(key_list[5], NTILES).astype(jnp.int32)
    return {"queries": queries, "key_states": key_states, "value_states": value_states, "block_lists": block_lists, "block_counts": block_counts, "tile_order": tile_order}


def reference(queries, key_states, value_states, block_lists, block_counts, tile_order):
    q_all = queries.reshape(NTILES, TILE, H, DH)
    k_all = key_states.reshape(NTILES, TILE, H, DH)
    v_all = value_states.reshape(NTILES, TILE, H, DH)
    slopes = 8.0 * jnp.power(2.0, -8.0 * jnp.arange(H).astype(jnp.float32) / H)
    scale = DH ** -0.5

    def one_tile(tile_index):
        listed = block_lists[tile_index]
        q_tile = q_all[tile_index].astype(jnp.float32)
        k_sel = k_all[listed].astype(jnp.float32)
        v_sel = v_all[listed].astype(jnp.float32)
        scores = jnp.einsum("ihd,cjhd->hicj", q_tile, k_sel) * scale
        distance = jnp.abs(tile_order[tile_index] - tile_order[listed]).astype(jnp.float32) / NTILES
        scores = scores - slopes[:, None, None, None] * distance[None, None, :, None]
        valid = jnp.arange(SLOTS, dtype=jnp.int32) < block_counts[tile_index]
        scores = jnp.where(valid[None, None, :, None], scores, -1e30).reshape(H, TILE, SLOTS * TILE)
        top = jnp.max(scores, axis=-1)
        weights = jnp.exp(scores - top[..., None]).astype(jnp.bfloat16)
        total = jnp.sum(weights.astype(jnp.float32), axis=-1)
        mixed = jnp.einsum("hik,khd->ihd", weights.astype(jnp.float32), v_sel.reshape(SLOTS * TILE, H, DH))
        return (mixed / total.T[:, :, None]).astype(jnp.bfloat16)

    result = lax.map(one_tile, jnp.arange(NTILES, dtype=jnp.int32))
    return result.reshape(SEQ, H * DH)
```

```python
import functools

import jax
import jax.numpy as jnp
import numpy as np
from jax import lax
from jax.experimental import pallas as pl
from jax.experimental.pallas import tpu as pltpu
from jax.sharding import PartitionSpec as P

H = 48
DH = 128
TILE = 128
REACH = 3
SLOTS = 8
GROUP = 8
HEADS = H // GROUP
META_ROWS = 8
MESH = pl.DeviceIdType.MESH


def kernel(
    blk_size,
    head_size,
    q_ref,
    k_ref,
    v_ref,
    meta_ref,
    order_ref,
    slope_ref,
    out_ref,
    *scratch,
):
    kv_bufs = scratch[:HEADS]
    (q_buf, o_buf, meta_v, meta_s, send_sem, near_sem, q_sem, far_sem, far_send_sem, out_send_sem, out_sem, meta_sem) = scratch[HEADS:]
    members = GROUP // head_size
    tps = head_size
    groups = blk_size // members
    side = REACH * tps
    hops = -(-REACH // members)

    blk = lax.axis_index("blk")
    head = lax.axis_index("head")
    group = blk // members
    place = blk % members
    mine = place * head_size + head

    def in_group(p):
        return {"blk": group * members + p // head_size, "head": p % head_size}

    def group_at(distance):
        return {"blk": (group + distance + groups) % groups * members + place, "head": head}

    far = []
    for hop in range(1, hops + 1):
        start = max(0, hop * members - REACH)
        far.append((hop, start * tps, (members - start) * tps, (start - hop * members + REACH) * tps))
        count = min(members, REACH - (hop - 1) * members)
        far.append((-hop, 0, count * tps, (hop * members + REACH) * tps))

    barrier = pltpu.get_barrier_semaphore()

    def greet(k, carry):
        pl.semaphore_signal(barrier, inc=1, device_id=in_group((mine + k) % GROUP), device_id_type=MESH)
        return carry

    lax.fori_loop(1, GROUP, greet, 0)
    for distance, *_ in far:
        pl.semaphore_signal(barrier, inc=1, device_id=group_at(distance), device_id_type=MESH)
    pl.semaphore_wait(barrier, GROUP - 1 + len(far))

    pltpu.make_async_copy(meta_ref, meta_v.at[place], meta_sem.at[0]).start()
    for k in range(1, members):
        pltpu.make_async_remote_copy(
            src_ref=meta_ref,
            dst_ref=meta_v.at[place],
            send_sem=meta_sem.at[1],
            recv_sem=meta_sem.at[0],
            device_id={"blk": group * members + (place + k) % members, "head": head},
            device_id_type=MESH,
        ).start()

    def columns(p, chunk):
        return pl.ds(pl.multiple_of((p * HEADS + chunk) * DH, DH), DH)

    def scatter(chunk, parts):
        for source, target, send, recv in parts:
            pltpu.make_async_copy(source.at[:, columns(mine, chunk)], target, recv).start()

        def to_peer(k, carry):
            p = (mine + k) % GROUP
            for source, target, send, recv in parts:
                pltpu.make_async_remote_copy(
                    src_ref=source.at[:, columns(p, chunk)],
                    dst_ref=target,
                    send_sem=send,
                    recv_sem=recv,
                    device_id=in_group(p),
                    device_id_type=MESH,
                ).start()
            return carry

        lax.fori_loop(1, GROUP, to_peer, 0)

    for chunk in range(HEADS):
        scatter(
            chunk,
            (
                (k_ref, kv_bufs[chunk].at[0, side + mine], send_sem.at[0], near_sem.at[chunk]),
                (v_ref, kv_bufs[chunk].at[1, side + mine], send_sem.at[1], near_sem.at[chunk]),
            ),
        )
    for chunk in range(HEADS):
        scatter(chunk, ((q_ref, q_buf.at[chunk, mine], send_sem.at[2], q_sem.at[chunk]),))

    for chunk in range(HEADS):
        own = kv_bufs[chunk].at[:, pl.ds(side, GROUP)]
        pltpu.make_async_copy(own, own, near_sem.at[chunk]).wait()
        for distance, first, tiles, there in far:
            pltpu.make_async_remote_copy(
                src_ref=kv_bufs[chunk].at[:, pl.ds(side + first, tiles)],
                dst_ref=kv_bufs[chunk].at[:, pl.ds(there, tiles)],
                send_sem=far_send_sem.at[chunk],
                recv_sem=far_sem.at[chunk],
                device_id=group_at(distance),
                device_id_type=MESH,
            ).start()

    pltpu.make_async_copy(meta_v, meta_v, meta_sem.at[0]).wait()
    to_scalar = pltpu.make_async_copy(meta_v, meta_s, meta_sem.at[2])
    to_scalar.start()
    to_scalar.wait()

    ones = jnp.ones((2 * TILE, DH), jnp.bfloat16)
    ntiles = order_ref.shape[0]
    scale = DH ** (-0.5)

    def attend(chunk):
        kv = kv_bufs[chunk]
        slope = slope_ref[mine * HEADS + chunk]

        def one_tile(k, carry):
            i = (mine + k) % GROUP
            q = q_buf[chunk, i]
            member, row = i // tps, i % tps
            count = meta_s[member, row, SLOTS]
            here = order_ref[group * GROUP + i]
            scores, values = [], []
            for c in range(SLOTS):
                u = meta_s[member, row, c]
                index = (u // tps - group * members + REACH + blk_size) % blk_size * tps + u % tps
                index = jnp.minimum(index, kv.shape[1] - 1)
                distance = jnp.abs(here - order_ref[u]).astype(jnp.float32) * (1.0 / ntiles)
                bias = jnp.where(c < count, slope * distance, 1e30)
                dots = lax.dot_general(
                    q, kv[0, index], (((1,), (1,)), ((), ())), preferred_element_type=jnp.float32
                )
                scores.append(dots * scale - bias)
                values.append(kv[1, index])
            top = functools.reduce(jnp.maximum, scores)
            top = jnp.max(top, axis=1, keepdims=True)
            mixed = jnp.zeros((TILE, 2 * DH), jnp.float32)
            for c in range(0, SLOTS, 2):
                weights = jnp.concatenate(
                    [jnp.exp(scores[c + e] - top).astype(jnp.bfloat16) for e in (0, 1)], axis=1
                )
                pair = jnp.concatenate([values[c], values[c + 1]], axis=0)
                mixed += jnp.dot(
                    weights,
                    jnp.concatenate([pair, ones], axis=1),
                    preferred_element_type=jnp.float32,
                )
            o_buf[chunk, i] = (mixed[:, :DH] / mixed[:, DH:]).astype(jnp.bfloat16)
            target = out_ref.at[:, columns(mine, chunk)]

            @pl.when(i == mine)
            def _():
                pltpu.make_async_copy(o_buf.at[chunk, i], target, out_sem).start()

            @pl.when(i != mine)
            def _():
                pltpu.make_async_remote_copy(
                    src_ref=o_buf.at[chunk, i],
                    dst_ref=target,
                    send_sem=out_send_sem,
                    recv_sem=out_sem,
                    device_id=in_group(i),
                    device_id_type=MESH,
                ).start()

            return carry

        lax.fori_loop(1, GROUP + 1, one_tile, 0)

    for chunk in range(HEADS):
        arrived = kv_bufs[chunk].at[:, pl.ds(0, 2 * side)]
        pltpu.make_async_copy(arrived, arrived, far_sem.at[chunk]).wait()
        pltpu.make_async_copy(q_buf.at[chunk], q_buf.at[chunk], q_sem.at[chunk]).wait()
        attend(chunk)

    sent = (GROUP - 1) * HEADS * DH
    for which, source in enumerate((k_ref, v_ref, q_ref)):
        part = source.at[:, pl.ds(0, sent)]
        pltpu.make_async_copy(part, part, send_sem.at[which]).wait()
    if members > 1:
        part = meta_v.at[pl.ds(0, members - 1)]
        pltpu.make_async_copy(part, part, meta_sem.at[1]).wait()
    for chunk in range(HEADS):
        arrived = kv_bufs[chunk].at[:, pl.ds(0, 2 * side)]
        pltpu.make_async_copy(arrived, arrived, far_send_sem.at[chunk]).wait()
    part = out_ref.at[:, pl.ds(0, sent)]
    pltpu.make_async_copy(part, part, out_send_sem).wait()
    pltpu.make_async_copy(out_ref, out_ref, out_sem).wait()


def body(queries, key_states, value_states, block_lists, block_counts, tile_order):
    blk_size = lax.axis_size("blk")
    head_size = lax.axis_size("head")
    members = GROUP // head_size
    window = GROUP + 2 * REACH * head_size
    meta = jnp.concatenate((block_lists, block_counts[:, None]), axis=1)
    meta = jnp.pad(meta, ((0, META_ROWS - meta.shape[0]), (0, 128 - meta.shape[1])))
    slopes = jnp.asarray(8.0 * 2.0 ** (-8.0 * np.arange(H) / H), jnp.float32)
    hbm = pl.BlockSpec(memory_space=pl.ANY)
    smem = pl.BlockSpec(memory_space=pltpu.SMEM)
    dma = pltpu.SemaphoreType.DMA
    return pl.pallas_call(
        functools.partial(kernel, blk_size, head_size),
        out_shape=jax.ShapeDtypeStruct(queries.shape, jnp.bfloat16),
        in_specs=[hbm, hbm, hbm, hbm, smem, smem],
        out_specs=hbm,
        scratch_shapes=[pltpu.VMEM((2, window, TILE, DH), jnp.bfloat16) for _ in range(HEADS)]
        + [
            pltpu.VMEM((HEADS, GROUP, TILE, DH), jnp.bfloat16),
            pltpu.VMEM((HEADS, GROUP, TILE, DH), jnp.bfloat16),
            pltpu.VMEM((members, META_ROWS, 128), jnp.int32),
            pltpu.SMEM((members, META_ROWS, 128), jnp.int32),
            dma((3,)),
            dma((HEADS,)),
            dma((HEADS,)),
            dma((HEADS,)),
            dma((HEADS,)),
            dma,
            dma,
            dma((3,)),
        ],
        compiler_params=pltpu.CompilerParams(
            collective_id=0, has_side_effects=True, vmem_limit_bytes=50 * 2**20
        ),
        cost_estimate=pl.CostEstimate(
            flops=4 * GROUP * HEADS * SLOTS * TILE * TILE * DH,
            bytes_accessed=8 * queries.size,
            transcendentals=GROUP * HEADS * SLOTS * TILE * TILE,
        ),
    )(queries, key_states, value_states, meta, tile_order, slopes)


def solution(mesh):
    in_specs = (
        P(("blk", "head"), None),
        P(("blk", "head"), None),
        P(("blk", "head"), None),
        P("blk", None),
        P("blk"),
        P(),
    )
    out_specs = P(("blk", "head"), None)
    return jax.shard_map(body, mesh=mesh, in_specs=in_specs, out_specs=out_specs, check_vma=False)
```

```python
import functools

import jax
import jax.numpy as jnp
from jax import lax
from jax.experimental import pallas as pl
from jax.experimental.pallas import tpu as pltpu
from jax.sharding import PartitionSpec as P

H = 48
DH = 128
TILE = 128
REACH = 3
SLOTS = 8
GROUP = 8
HEADS = H // GROUP
META_ROWS = 8
MESH = pl.DeviceIdType.MESH


def kernel(
    blk_size,
    head_size,
    q_ref,
    k_ref,
    v_ref,
    lists_ref,
    counts_ref,
    order_ref,
    out_ref,
    *scratch,
):
    kv_bufs = scratch[:HEADS]
    (q_buf, o_buf, meta_v, meta_s, send_sem, near_sem, q_sem, far_sem, far_send_sem, out_send_sem, out_sem, meta_sem) = scratch[HEADS:]
    members = GROUP // head_size
    tps = head_size
    groups = blk_size // members
    side = REACH * tps
    hops = -(-REACH // members)

    blk = lax.axis_index("blk")
    head = lax.axis_index("head")
    group = blk // members
    place = blk % members
    mine = place * head_size + head

    def in_group(p):
        return {"blk": group * members + p // head_size, "head": p % head_size}

    def group_at(distance):
        return {"blk": (group + distance + groups) % groups * members + place, "head": head}

    far = []
    for hop in range(1, hops + 1):
        start = max(0, hop * members - REACH)
        far.append((hop, start * tps, (members - start) * tps, (start - hop * members + REACH) * tps))
        count = min(members, REACH - (hop - 1) * members)
        far.append((-hop, 0, count * tps, (hop * members + REACH) * tps))

    barrier = pltpu.get_barrier_semaphore()

    def greet(k, carry):
        pl.semaphore_signal(barrier, inc=1, device_id=in_group((mine + k) % GROUP), device_id_type=MESH)
        return carry

    lax.fori_loop(1, GROUP, greet, 0)
    for distance, *_ in far:
        pl.semaphore_signal(barrier, inc=1, device_id=group_at(distance), device_id_type=MESH)
    pl.semaphore_wait(barrier, GROUP - 1 + len(far))

    rows = lax.broadcasted_iota(jnp.int32, (META_ROWS, 128), 0)
    lanes = lax.broadcasted_iota(jnp.int32, (META_ROWS, 128), 1)
    meta = jnp.zeros((META_ROWS, 128), jnp.int32)
    for r in range(tps):
        for c in range(SLOTS + 1):
            item = lists_ref[r, c] if c < SLOTS else counts_ref[r]
            meta = jnp.where((rows == r) & (lanes == c), item, meta)
    meta_v[place] = meta
    for k in range(1, members):
        pltpu.make_async_remote_copy(
            src_ref=meta_v.at[place],
            dst_ref=meta_v.at[place],
            send_sem=meta_sem.at[1],
            recv_sem=meta_sem.at[0],
            device_id={"blk": group * members + (place + k) % members, "head": head},
            device_id_type=MESH,
        ).start()

    def columns(p, chunk):
        return pl.ds(pl.multiple_of((p * HEADS + chunk) * DH, DH), DH)

    def scatter(chunk, parts):
        for source, target, send, recv in parts:
            pltpu.make_async_copy(source.at[:, columns(mine, chunk)], target, recv).start()

        def to_peer(k, carry):
            p = (mine + k) % GROUP
            for source, target, send, recv in parts:
                pltpu.make_async_remote_copy(
                    src_ref=source.at[:, columns(p, chunk)],
                    dst_ref=target,
                    send_sem=send,
                    recv_sem=recv,
                    device_id=in_group(p),
                    device_id_type=MESH,
                ).start()
            return carry

        lax.fori_loop(1, GROUP, to_peer, 0)

    def own_tile(chunk):
        for distance, first, tiles, there in far:

            @pl.when((mine >= first) & (mine < first + tiles))
            def _():
                for e, source in enumerate((k_ref, v_ref)):
                    pltpu.make_async_remote_copy(
                        src_ref=source.at[:, columns(mine, chunk)],
                        dst_ref=kv_bufs[chunk].at[e, there - first + mine],
                        send_sem=far_send_sem.at[chunk],
                        recv_sem=far_sem.at[chunk],
                        device_id=group_at(distance),
                        device_id_type=MESH,
                    ).start()

    for chunk in range(HEADS):
        own_tile(chunk)
        scatter(
            chunk,
            (
                (k_ref, kv_bufs[chunk].at[0, side + mine], send_sem.at[0], near_sem.at[chunk]),
                (v_ref, kv_bufs[chunk].at[1, side + mine], send_sem.at[1], near_sem.at[chunk]),
            ),
        )
    for chunk in range(HEADS):
        own = kv_bufs[chunk].at[:, pl.ds(side, GROUP)]
        pltpu.make_async_copy(own, own, near_sem.at[chunk]).wait()

        def pass_on(k, carry):
            p = (mine + k) % GROUP
            for distance, first, tiles, there in far:

                @pl.when((p >= first) & (p < first + tiles))
                def _():
                    pltpu.make_async_remote_copy(
                        src_ref=kv_bufs[chunk].at[:, side + p],
                        dst_ref=kv_bufs[chunk].at[:, there - first + p],
                        send_sem=far_send_sem.at[chunk],
                        recv_sem=far_sem.at[chunk],
                        device_id=group_at(distance),
                        device_id_type=MESH,
                    ).start()

            return carry

        lax.fori_loop(1, GROUP, pass_on, 0)
        scatter(chunk, ((q_ref, q_buf.at[chunk, mine], send_sem.at[2], q_sem.at[chunk]),))

    if members > 1:
        part = meta_v.at[pl.ds(0, members - 1)]
        pltpu.make_async_copy(part, part, meta_sem.at[0]).wait()
    to_scalar = pltpu.make_async_copy(meta_v, meta_s, meta_sem.at[2])
    to_scalar.start()
    to_scalar.wait()

    ones = jnp.ones((2 * TILE, DH), jnp.bfloat16)
    ntiles = order_ref.shape[0]
    scale = DH ** (-0.5)

    def attend(chunk):
        kv = kv_bufs[chunk]
        slope = (1 << (GROUP - 1 - mine)).astype(jnp.float32) * (
            8.0 * 2.0 ** (-8.0 * chunk / H) / 2 ** (GROUP - 1) / ntiles
        )

        def one_tile(i):
            q = q_buf[chunk, i]
            member, row = i // tps, i % tps
            count = meta_s[member, row, SLOTS]
            here = order_ref[group * GROUP + i]
            places, biases = [], []
            for c in range(SLOTS):
                u = meta_s[member, row, c]
                index = (u // tps - group * members + REACH + blk_size) % blk_size * tps + u % tps
                places.append(jnp.minimum(index, kv.shape[1] - 1))
                distance = jnp.abs(here - order_ref[u]).astype(jnp.float32)
                biases.append(jnp.where(c < count, slope * distance, 1e30))
            scores = []
            for c in range(0, SLOTS, 2):
                pair = jnp.concatenate([kv[0, places[c]], kv[0, places[c + 1]]], axis=0)
                dots = lax.dot_general(
                    q, pair, (((1,), (1,)), ((), ())), preferred_element_type=jnp.float32
                )
                for e in (0, 1):
                    scores.append(dots[:, e * TILE : (e + 1) * TILE] * scale - biases[c + e])
            top = functools.reduce(jnp.maximum, scores)
            top = jnp.max(top, axis=1, keepdims=True)
            mixed = jnp.zeros((TILE, 2 * DH), jnp.float32)
            for c in range(0, SLOTS, 2):
                weights = jnp.concatenate(
                    [jnp.exp(scores[c + e] - top).astype(jnp.bfloat16) for e in (0, 1)], axis=1
                )
                pair = jnp.concatenate([kv[1, places[c]], kv[1, places[c + 1]]], axis=0)
                mixed += jnp.dot(
                    weights,
                    jnp.concatenate([pair, ones], axis=1),
                    preferred_element_type=jnp.float32,
                )
            return (mixed[:, :DH] / mixed[:, DH:]).astype(jnp.bfloat16)

        target = out_ref.at[:, columns(mine, chunk)]

        def send(i):
            @pl.when(i == mine)
            def _():
                pltpu.make_async_copy(o_buf.at[chunk, i], target, out_sem).start()

            @pl.when(i != mine)
            def _():
                pltpu.make_async_remote_copy(
                    src_ref=o_buf.at[chunk, i],
                    dst_ref=target,
                    send_sem=out_send_sem,
                    recv_sem=out_sem,
                    device_id=in_group(i),
                    device_id_type=MESH,
                ).start()

        def two_tiles(k, carry):
            pair = [(mine + 1 + 2 * k + e) % GROUP for e in (0, 1)]
            results = [one_tile(i) for i in pair]
            for i, result in zip(pair, results):
                o_buf[chunk, i] = result
            for i in pair:
                send(i)
            return carry

        lax.fori_loop(0, GROUP // 2, two_tiles, 0)

    for chunk in range(HEADS):
        arrived = kv_bufs[chunk].at[:, pl.ds(0, 2 * side)]
        pltpu.make_async_copy(arrived, arrived, far_sem.at[chunk]).wait()
        pltpu.make_async_copy(q_buf.at[chunk], q_buf.at[chunk], q_sem.at[chunk]).wait()
        attend(chunk)

    sent = (GROUP - 1) * HEADS * DH
    for which, source in enumerate((k_ref, v_ref, q_ref)):
        part = source.at[:, pl.ds(0, sent)]
        pltpu.make_async_copy(part, part, send_sem.at[which]).wait()
    if members > 1:
        part = meta_v.at[pl.ds(0, members - 1)]
        pltpu.make_async_copy(part, part, meta_sem.at[1]).wait()
    for chunk in range(HEADS):
        arrived = kv_bufs[chunk].at[:, pl.ds(0, 2 * side)]
        pltpu.make_async_copy(arrived, arrived, far_send_sem.at[chunk]).wait()
    part = out_ref.at[:, pl.ds(0, sent)]
    pltpu.make_async_copy(part, part, out_send_sem).wait()
    pltpu.make_async_copy(out_ref, out_ref, out_sem).wait()


def body(queries, key_states, value_states, block_lists, block_counts, tile_order):
    blk_size = lax.axis_size("blk")
    head_size = lax.axis_size("head")
    members = GROUP // head_size
    window = GROUP + 2 * REACH * head_size
    hbm = pl.BlockSpec(memory_space=pl.ANY)
    smem = pl.BlockSpec(memory_space=pltpu.SMEM)
    dma = pltpu.SemaphoreType.DMA
    return pl.pallas_call(
        functools.partial(kernel, blk_size, head_size),
        out_shape=jax.ShapeDtypeStruct(queries.shape, jnp.bfloat16),
        in_specs=[hbm, hbm, hbm, smem, smem, smem],
        out_specs=hbm,
        scratch_shapes=[pltpu.VMEM((2, window, TILE, DH), jnp.bfloat16) for _ in range(HEADS)]
        + [
            pltpu.VMEM((HEADS, GROUP, TILE, DH), jnp.bfloat16),
            pltpu.VMEM((HEADS, GROUP, TILE, DH), jnp.bfloat16),
            pltpu.VMEM((members, META_ROWS, 128), jnp.int32),
            pltpu.SMEM((members, META_ROWS, 128), jnp.int32),
            dma((3,)),
            dma((HEADS,)),
            dma((HEADS,)),
            dma((HEADS,)),
            dma((HEADS,)),
            dma,
            dma,
            dma((3,)),
        ],
        compiler_params=pltpu.CompilerParams(
            collective_id=0, has_side_effects=True, vmem_limit_bytes=63 * 2**20
        ),
        cost_estimate=pl.CostEstimate(
            flops=4 * GROUP * HEADS * SLOTS * TILE * TILE * DH,
            bytes_accessed=8 * queries.size,
            transcendentals=GROUP * HEADS * SLOTS * TILE * TILE,
        ),
    )(queries, key_states, value_states, block_lists, block_counts, tile_order)


def solution(mesh):
    in_specs = (
        P(("blk", "head"), None),
        P(("blk", "head"), None),
        P(("blk", "head"), None),
        P("blk", None),
        P("blk"),
        P(),
    )
    out_specs = P(("blk", "head"), None)
    return jax.shard_map(body, mesh=mesh, in_specs=in_specs, out_specs=out_specs, check_vma=False)
```

```python
import functools

import jax
import jax.numpy as jnp
from jax import lax
from jax.experimental import pallas as pl
from jax.experimental.pallas import tpu as pltpu
from jax.sharding import PartitionSpec as P

H = 48
DH = 128
TILE = 128
REACH = 3
SLOTS = 8
GROUP = 8
HEADS = H // GROUP
META_ROWS = 8
MESH = pl.DeviceIdType.MESH


def kernel(
    blk_size,
    head_size,
    q_ref,
    k_ref,
    v_ref,
    lists_ref,
    counts_ref,
    order_ref,
    out_ref,
    *scratch,
):
    kv_bufs = [(ref,) for ref in scratch[: HEADS - 1]] + [scratch[HEADS - 1 : HEADS + 1]]
    (q_buf, o_buf, w_buf, meta_v, meta_s, send_sem, near_sem, q_sem, far_sem, far_send_sem, out_send_sem, out_sem, meta_sem) = scratch[HEADS + 1 :]
    members = GROUP // head_size
    tps = head_size
    groups = blk_size // members
    side = REACH * tps
    hops = -(-REACH // members)

    blk = lax.axis_index("blk")
    head = lax.axis_index("head")
    group = blk // members
    place = blk % members
    mine = place * head_size + head

    def in_group(p):
        return {"blk": group * members + p // head_size, "head": p % head_size}

    def group_at(distance):
        return {"blk": (group + distance + groups) % groups * members + place, "head": head}

    far = []
    for hop in range(1, hops + 1):
        start = max(0, hop * members - REACH)
        far.append((hop, start * tps, (members - start) * tps, (start - hop * members + REACH) * tps))
        count = min(members, REACH - (hop - 1) * members)
        far.append((-hop, 0, count * tps, (hop * members + REACH) * tps))

    barrier = pltpu.get_barrier_semaphore()

    def greet(k, carry):
        pl.semaphore_signal(barrier, inc=1, device_id=in_group((mine + k) % GROUP), device_id_type=MESH)
        return carry

    lax.fori_loop(1, GROUP, greet, 0)
    for distance, *_ in far:
        pl.semaphore_signal(barrier, inc=1, device_id=group_at(distance), device_id_type=MESH)
    pl.semaphore_wait(barrier, GROUP - 1 + len(far))

    rows = lax.broadcasted_iota(jnp.int32, (META_ROWS, 128), 0)
    lanes = lax.broadcasted_iota(jnp.int32, (META_ROWS, 128), 1)
    meta = jnp.zeros((META_ROWS, 128), jnp.int32)
    for r in range(tps):
        for c in range(SLOTS + 1):
            item = lists_ref[r, c] if c < SLOTS else counts_ref[r]
            meta = jnp.where((rows == r) & (lanes == c), item, meta)
    meta_v[place] = meta
    for k in range(1, members):
        pltpu.make_async_remote_copy(
            src_ref=meta_v.at[place],
            dst_ref=meta_v.at[place],
            send_sem=meta_sem.at[1],
            recv_sem=meta_sem.at[0],
            device_id={"blk": group * members + (place + k) % members, "head": head},
            device_id_type=MESH,
        ).start()

    def half(chunk, e):
        bufs = kv_bufs[chunk]
        return bufs[0].at[e] if len(bufs) == 1 else bufs[e].at[0]

    def sem_of(chunk, e):
        return chunk + e if len(kv_bufs[chunk]) > 1 else chunk

    def columns(p, chunk):
        return pl.ds(pl.multiple_of((p * HEADS + chunk) * DH, DH), DH)

    def scatter(chunk, parts):
        for source, target, send, recv in parts:
            pltpu.make_async_copy(source.at[:, columns(mine, chunk)], target, recv).start()

        def to_peer(k, carry):
            p = (mine + k) % GROUP
            for source, target, send, recv in parts:
                pltpu.make_async_remote_copy(
                    src_ref=source.at[:, columns(p, chunk)],
                    dst_ref=target,
                    send_sem=send,
                    recv_sem=recv,
                    device_id=in_group(p),
                    device_id_type=MESH,
                ).start()
            return carry

        lax.fori_loop(1, GROUP, to_peer, 0)

    def own_tile(chunk):
        for distance, first, tiles, there in far:

            @pl.when((mine >= first) & (mine < first + tiles))
            def _():
                for e, source in enumerate((k_ref, v_ref)):
                    pltpu.make_async_remote_copy(
                        src_ref=source.at[:, columns(mine, chunk)],
                        dst_ref=half(chunk, e).at[there - first + mine],
                        send_sem=far_send_sem.at[sem_of(chunk, e)],
                        recv_sem=far_sem.at[sem_of(chunk, e)],
                        device_id=group_at(distance),
                        device_id_type=MESH,
                    ).start()

    for chunk in range(HEADS):
        own_tile(chunk)
        scatter(
            chunk,
            (
                (k_ref, half(chunk, 0).at[side + mine], send_sem.at[0], near_sem.at[sem_of(chunk, 0)]),
                (v_ref, half(chunk, 1).at[side + mine], send_sem.at[1], near_sem.at[sem_of(chunk, 1)]),
            ),
        )
    def pass_on(buf, which):
        own = buf.at[:, pl.ds(side, GROUP)]
        pltpu.make_async_copy(own, own, near_sem.at[which]).wait()

        def one_place(k, carry):
            p = (mine + k) % GROUP
            for distance, first, tiles, there in far:

                @pl.when((p >= first) & (p < first + tiles))
                def _():
                    pltpu.make_async_remote_copy(
                        src_ref=buf.at[:, side + p],
                        dst_ref=buf.at[:, there - first + p],
                        send_sem=far_send_sem.at[which],
                        recv_sem=far_sem.at[which],
                        device_id=group_at(distance),
                        device_id_type=MESH,
                    ).start()

            return carry

        lax.fori_loop(1, GROUP, one_place, 0)

    for chunk in range(HEADS):
        for e, buf in enumerate(kv_bufs[chunk]):
            pass_on(buf, sem_of(chunk, e))
        scatter(chunk, ((q_ref, q_buf.at[chunk, mine], send_sem.at[2], q_sem.at[chunk]),))

    if members > 1:
        part = meta_v.at[pl.ds(0, members - 1)]
        pltpu.make_async_copy(part, part, meta_sem.at[0]).wait()
    to_scalar = pltpu.make_async_copy(meta_v, meta_s, meta_sem.at[2])
    to_scalar.start()
    to_scalar.wait()

    ones = jnp.ones((2 * TILE, DH), jnp.bfloat16)
    ntiles = order_ref.shape[0]
    scale = DH ** (-0.5)

    def window_place(i, c):
        u = meta_s[i // tps, i % tps, c]
        index = (u // tps - group * members + REACH + blk_size) % blk_size * tps + u % tps
        return jnp.minimum(index, 2 * side + GROUP - 1)

    def arrive(chunk, e):
        buf = kv_bufs[chunk][e]
        arrived = buf.at[:, pl.ds(0, 2 * side)]
        pltpu.make_async_copy(arrived, arrived, far_sem.at[sem_of(chunk, e)]).wait()

    def attend(chunk):
        bufs = kv_bufs[chunk]

        def key_tile(index):
            return bufs[0][0, index]

        def value_tile(index):
            return bufs[0][1, index] if len(bufs) == 1 else bufs[1][0, index]

        slope = (1 << (GROUP - 1 - mine)).astype(jnp.float32) * (
            8.0 * 2.0 ** (-8.0 * chunk / H) / 2 ** (GROUP - 1) / ntiles
        )

        def weigh(i):
            q = q_buf[chunk, i]
            count = meta_s[i // tps, i % tps, SLOTS]
            here = order_ref[group * GROUP + i]
            biases = []
            for c in range(SLOTS):
                u = meta_s[i // tps, i % tps, c]
                distance = jnp.abs(here - order_ref[u]).astype(jnp.float32)
                biases.append(jnp.where(c < count, slope * distance, 1e30))
            scores = []
            for c in range(0, SLOTS, 2):
                pair = jnp.concatenate([key_tile(window_place(i, c + e)) for e in (0, 1)], axis=0)
                dots = lax.dot_general(
                    q, pair, (((1,), (1,)), ((), ())), preferred_element_type=jnp.float32
                )
                for e in (0, 1):
                    scores.append(dots[:, e * TILE : (e + 1) * TILE] * scale - biases[c + e])
            top = functools.reduce(jnp.maximum, scores)
            top = jnp.max(top, axis=1, keepdims=True)
            return [
                jnp.concatenate(
                    [jnp.exp(scores[c + e] - top).astype(jnp.bfloat16) for e in (0, 1)], axis=1
                )
                for c in range(0, SLOTS, 2)
            ]

        def mix(i, weights):
            mixed = jnp.zeros((TILE, 2 * DH), jnp.float32)
            for c in range(0, SLOTS, 2):
                pair = jnp.concatenate([value_tile(window_place(i, c + e)) for e in (0, 1)], axis=0)
                mixed += jnp.dot(
                    weights[c // 2],
                    jnp.concatenate([pair, ones], axis=1),
                    preferred_element_type=jnp.float32,
                )
            return (mixed[:, :DH] / mixed[:, DH:]).astype(jnp.bfloat16)

        target = out_ref.at[:, columns(mine, chunk)]

        def send(i):
            @pl.when(i == mine)
            def _():
                pltpu.make_async_copy(o_buf.at[chunk, i], target, out_sem).start()

            @pl.when(i != mine)
            def _():
                pltpu.make_async_remote_copy(
                    src_ref=o_buf.at[chunk, i],
                    dst_ref=target,
                    send_sem=out_send_sem,
                    recv_sem=out_sem,
                    device_id=in_group(i),
                    device_id_type=MESH,
                ).start()

        def pair_at(k):
            return [(mine + 1 + 2 * k + e) % GROUP for e in (0, 1)]

        def finish(pair, results):
            for i, result in zip(pair, results):
                o_buf[chunk, i] = result
            for i in pair:
                send(i)

        if len(bufs) == 1:

            def two_tiles(k, carry):
                pair = pair_at(k)
                finish(pair, [mix(i, weigh(i)) for i in pair])
                return carry

            lax.fori_loop(0, GROUP // 2, two_tiles, 0)
            return

        def two_weights(k, carry):
            pair = pair_at(k)
            for i, weights in zip(pair, [weigh(i) for i in pair]):
                for part in range(SLOTS // 2):
                    w_buf[i, part] = weights[part]
            return carry

        def two_mixes(k, carry):
            pair = pair_at(k)
            finish(pair, [mix(i, [w_buf[i, part] for part in range(SLOTS // 2)]) for i in pair])
            return carry

        lax.fori_loop(0, GROUP // 2, two_weights, 0)
        arrive(chunk, 1)
        lax.fori_loop(0, GROUP // 2, two_mixes, 0)

    for chunk in range(HEADS):
        arrive(chunk, 0)
        pltpu.make_async_copy(q_buf.at[chunk], q_buf.at[chunk], q_sem.at[chunk]).wait()
        attend(chunk)

    sent = (GROUP - 1) * HEADS * DH
    for which, source in enumerate((k_ref, v_ref, q_ref)):
        part = source.at[:, pl.ds(0, sent)]
        pltpu.make_async_copy(part, part, send_sem.at[which]).wait()
    if members > 1:
        part = meta_v.at[pl.ds(0, members - 1)]
        pltpu.make_async_copy(part, part, meta_sem.at[1]).wait()
    for chunk in range(HEADS):
        for e, buf in enumerate(kv_bufs[chunk]):
            passed = buf.at[:, pl.ds(0, 2 * side)]
            pltpu.make_async_copy(passed, passed, far_send_sem.at[sem_of(chunk, e)]).wait()
    part = out_ref.at[:, pl.ds(0, sent)]
    pltpu.make_async_copy(part, part, out_send_sem).wait()
    pltpu.make_async_copy(out_ref, out_ref, out_sem).wait()


def body(queries, key_states, value_states, block_lists, block_counts, tile_order):
    blk_size = lax.axis_size("blk")
    head_size = lax.axis_size("head")
    members = GROUP // head_size
    window = GROUP + 2 * REACH * head_size
    hbm = pl.BlockSpec(memory_space=pl.ANY)
    smem = pl.BlockSpec(memory_space=pltpu.SMEM)
    dma = pltpu.SemaphoreType.DMA
    return pl.pallas_call(
        functools.partial(kernel, blk_size, head_size),
        out_shape=jax.ShapeDtypeStruct(queries.shape, jnp.bfloat16),
        in_specs=[hbm, hbm, hbm, smem, smem, smem],
        out_specs=hbm,
        scratch_shapes=[pltpu.VMEM((2, window, TILE, DH), jnp.bfloat16) for _ in range(HEADS - 1)]
        + [pltpu.VMEM((1, window, TILE, DH), jnp.bfloat16) for _ in range(2)]
        + [
            pltpu.VMEM((HEADS, GROUP, TILE, DH), jnp.bfloat16),
            pltpu.VMEM((HEADS, GROUP, TILE, DH), jnp.bfloat16),
            pltpu.VMEM((GROUP, SLOTS // 2, TILE, 2 * TILE), jnp.bfloat16),
            pltpu.VMEM((members, META_ROWS, 128), jnp.int32),
            pltpu.SMEM((members, META_ROWS, 128), jnp.int32),
            dma((3,)),
            dma((HEADS + 1,)),
            dma((HEADS,)),
            dma((HEADS + 1,)),
            dma((HEADS + 1,)),
            dma,
            dma,
            dma((3,)),
        ],
        compiler_params=pltpu.CompilerParams(
            collective_id=0, has_side_effects=True, vmem_limit_bytes=63 * 2**20
        ),
        cost_estimate=pl.CostEstimate(
            flops=4 * GROUP * HEADS * SLOTS * TILE * TILE * DH,
            bytes_accessed=8 * queries.size,
            transcendentals=GROUP * HEADS * SLOTS * TILE * TILE,
        ),
    )(queries, key_states, value_states, block_lists, block_counts, tile_order)


def solution(mesh):
    in_specs = (
        P(("blk", "head"), None),
        P(("blk", "head"), None),
        P(("blk", "head"), None),
        P("blk", None),
        P("blk"),
        P(),
    )
    out_specs = P(("blk", "head"), None)
    return jax.shard_map(body, mesh=mesh, in_specs=in_specs, out_specs=out_specs, check_vma=False)
```
